32 devices in a mesh: groups: 2 (over y), nodes: 4 (over z), classes: 4 (over x, core).
Axes of the slice: x: 2, y: 2, z: 4, core: 2. Of those that a mesh axis runs over, the one named last changes fastest.
Arguments:
- scores: float32 [1024, 8192], P('classes', ('groups', 'nodes')), parts along dimension 1, may hold values from 0.2 to 15, as said below
- prior: float32 [1024, 8192], P('classes', ('groups', 'nodes')), parts along dimension 1, may hold values from 0 to 2
- tiles: bfloat16 [8, 4, 6, 128, 128], P(('groups', 'nodes')), parts along dimension 0, may hold values from 0 to 0.015625
- col_tile: int32 [8, 4, 6], P(('groups', 'nodes')), parts along dimension 0, may hold values from 0 to 7
- row_tile: int32 [8, 4, 6], P('groups', 'nodes'), parts along dimension 0, may hold values from 0 to 7
- counts: int32 [8, 4], P('groups', 'nodes'), parts along dimension 0, may hold values from 1 to 6, as said below
- seed_mask: int32 [8192], P(('groups', 'nodes')), parts along dimension 0, may hold values 0 or 1
Outputs:
- spread_scores: float32 [1024, 8192], P('classes', ('groups', 'nodes')), parts along dimension 1
The draws below stay inside these ranges and needn't reach their ends.
There are 2 independent parts, one for each index of `groups`. The reference program is written for one: setup_inputs(seed, part) draws one part's arguments, and reference() takes and returns one part's arrays. A program takes and returns all parts, laid end to end along the dimension named above; each array names one. Nothing has to cross between parts.
Inputs may be any that keep to these rules, and one draw needn't show every extreme that they name: Each node's starting scores are positive. counts[p, d] slots of the 6 from partition p to partition d are used; in every draw some partition receives 6 from every partition.
All inputs are finite; a program needn't handle non-finite values. No bound on the sum of `seed_mask` on one device may be relied on, other than what follows from the above.
Results may differ from the reference program's by a relative error of at most 0.0003.
Values may be sent and summed in bfloat16 or wider, within the bound.
A program may use at most 64 MiB of HBM per device.

```python
import math
import jax
import jax.numpy as jnp
from jax import lax

CLASSES = 1024
TILE = 128
NB = 8
CAP = 6
ITERS = 2
PARTITIONS = 4
NODES = 4096


def draw_scores(key, part):
    key = jax.random.fold_in(key, 11)
    ranking = jnp.arange(CLASSES, dtype=jnp.float32)[:, None] / CLASSES
    rising = jnp.exp(ranking * math.log(3.0))
    base = jnp.exp(jax.random.uniform(key, (CLASSES, NODES), jnp.float32, -1.5, 1.5))
    return (base * rising).astype(jnp.float32)


def draw_counts(key, part):
    key = jax.random.fold_in(key, 23)
    first_key, second_key = jax.random.split(key)
    base = jax.random.randint(first_key, (PARTITIONS, PARTITIONS), 1, CAP + 1)
    heavy = jax.random.randint(second_key, (), 0, PARTITIONS)
    column = jnp.arange(PARTITIONS, dtype=jnp.int32)[None, :] == heavy
    return jnp.where(column, CAP, base).astype(jnp.int32)


def set_ends(drawn, rng, low, largest):
    index_at = [jax.random.randint(jax.random.fold_in(rng, axis), (), 0, length) for axis, length in enumerate(drawn.shape)]
    main_axis = drawn.shape.index(max(drawn.shape))
    neighbour = index_at[:main_axis] + [(index_at[main_axis] + 1) % drawn.shape[main_axis]] + index_at[main_axis + 1:]
    return drawn.at[tuple(index_at)].set(low).at[tuple(neighbour)].set(largest)


def block_levels(stream_key, dims, pieces, smallest, largest):
    def one(axis_at, parts):
        heights = jax.random.uniform(jax.random.fold_in(jax.random.fold_in(stream_key, 6), axis_at), (parts,), jnp.float32, smallest / len(pieces), largest / len(pieces))
        return jnp.repeat(jnp.exp(heights), dims[axis_at] // parts).reshape((-1,) + (1,) * (len(dims) - axis_at - 1))

    factor_of = one(*pieces[0])
    for cut in pieces[1:]:
        factor_of = factor_of * one(*cut)
    return factor_of


def setup_inputs(seed: int = 0, part: int = 0) -> dict:
    arg_keys = jax.random.split(jax.random.key(seed), 8)
    part_keys = jax.random.split(jax.random.fold_in(arg_keys[7], part), 8)
    scores = draw_scores(jax.random.fold_in(jax.random.fold_in(arg_keys[7], part), 71), part)
    prior = jnp.clip(2.0 * jax.random.uniform(part_keys[1], (CLASSES, NODES), jnp.float32) ** block_levels(part_keys[1], (CLASSES, NODES), ((0, 4), (1, 4)), -0.2, 0.2), 0.0, 2.0)
    tiles = jnp.clip(0.015625 * jax.random.uniform(part_keys[2], (PARTITIONS, PARTITIONS, CAP, TILE, TILE), jnp.float32) ** block_levels(part_keys[2], (PARTITIONS, PARTITIONS, CAP, TILE, TILE), ((0, 4),), -0.2, 0.2), 0.0, 0.015625).astype(jnp.bfloat16)
    col_tile = set_ends(jax.random.randint(part_keys[3], (PARTITIONS, PARTITIONS, CAP), 0, NB), jax.random.fold_in(part_keys[3], 1), 0, NB - 1).astype(jnp.int32)
    row_tile = set_ends(jax.random.randint(part_keys[4], (PARTITIONS, PARTITIONS, CAP), 0, NB), jax.random.fold_in(part_keys[4], 1), 0, NB - 1).astype(jnp.int32)
    counts = draw_counts(jax.random.fold_in(jax.random.fold_in(arg_keys[7], part), 71), part)
    seed_mask = set_ends((jax.random.randint(part_keys[6], (NODES,), 0, 2) < 1).astype(jnp.int32), jax.random.fold_in(part_keys[6], 1), 0, 1)
    return dict(scores=scores, prior=prior, tiles=tiles, col_tile=col_tile, row_tile=row_tile, counts=counts, seed_mask=seed_mask)


def reference(scores, prior, tiles, col_tile, row_tile, counts, seed_mask):
    partition_count = tiles.shape[0]
    slot_count = tiles.shape[2]
    tile_width = tiles.shape[3]
    class_count = scores.shape[0]
    block_count = scores.shape[1] // (partition_count * tile_width)
    usable = jnp.arange(slot_count, dtype=jnp.int32)[None, None, :] < counts[:, :, None]
    seeded = seed_mask.astype(jnp.float32)[None, :]
    scores_now = scores

    def one_source(running, inputs):
        source_low, source_tiles, source_cols, source_rows, source_usable = inputs
        picked = jnp.take(source_low, source_cols, axis=1)
        products = jnp.einsum('cdsk,dskj->dscj', picked.astype(jnp.float32), source_tiles.astype(jnp.float32))
        products = products.astype(jnp.bfloat16).astype(jnp.float32)
        placing = jax.nn.one_hot(source_rows, block_count, dtype=jnp.float32) * source_usable[..., None].astype(jnp.float32)
        running = running + jnp.einsum('dsb,dscj->cdbj', placing, products)
        return running, None

    for sweep in range(ITERS):
        field_low = scores_now.astype(jnp.bfloat16).reshape(class_count, partition_count, block_count, tile_width)
        field_low = jnp.moveaxis(field_low, 1, 0)
        start = jnp.zeros((class_count, partition_count, block_count, tile_width), jnp.float32)
        received, unused = lax.scan(one_source, start, (field_low, tiles, col_tile, row_tile, usable))
        tallied = scores_now + received.reshape(class_count, -1)
        node_total = jnp.sum(tallied, axis=0)
        normed = CLASSES * tallied / node_total[None, :]
        scores_now = normed + 0.5 * seeded * (prior - normed)
    return scores_now
```

```python
import functools

import jax
import jax.numpy as jnp
from jax import lax
from jax.experimental import pallas as pl
from jax.experimental.pallas import tpu as pltpu
from jax.sharding import PartitionSpec as P

CLASSES = 1024
ITERS = 2
MESH = pl.DeviceIdType.MESH
F32 = jnp.float32
I32 = jnp.int32


def body(scores, prior, tiles, col_tile, row_tile, counts, seed_mask):
    tiles = tiles[0]
    col_tile = col_tile[0]
    incoming_rows = row_tile[:, 0]
    incoming_counts = counts[:, 0]
    tile_width = tiles.shape[-1]
    class_rows = scores.shape[0]
    block_count = scores.shape[1] // tile_width
    usable = lax.broadcasted_iota(jnp.int32, incoming_rows.shape, 1) < incoming_counts[:, None]
    target_pick = jax.nn.one_hot(incoming_rows, block_count, dtype=jnp.bfloat16) * usable[
        ..., None
    ].astype(jnp.bfloat16)
    source_pick = jax.nn.one_hot(col_tile, block_count, dtype=jnp.bfloat16)
    seeded = seed_mask.astype(jnp.float32)[None, :]
    scores_now = scores
    for sweep in range(ITERS):
        field_low = scores_now.astype(jnp.bfloat16).reshape(class_rows, block_count, tile_width)
        picked = jnp.einsum(
            "pse,cek->psck", source_pick, field_low, preferred_element_type=jnp.float32
        ).astype(jnp.bfloat16)
        products = jnp.einsum(
            "psck,pskj->pscj", picked, tiles, preferred_element_type=jnp.float32
        ).astype(jnp.bfloat16)
        arrived = lax.all_to_all(products, "nodes", split_axis=0, concat_axis=0, tiled=True)
        gathered = jnp.einsum(
            "pse,pscj->cej", target_pick, arrived, preferred_element_type=jnp.float32
        )
        tallied = scores_now + gathered.reshape(class_rows, block_count * tile_width)
        node_total = lax.psum(jnp.sum(tallied, axis=0), "classes")
        normed = CLASSES * tallied / node_total[None, :]
        scores_now = normed + 0.5 * seeded * (prior - normed)
    return scores_now


def pack(codes):
    half = codes.shape[0] // 2
    return lax.bitwise_or(codes[:half], lax.shift_left(codes[half:], jnp.int32(16)))


def unpack(words):
    low = lax.bitwise_and(words, jnp.int32(0xFFFF))
    high = lax.shift_right_logical(words, jnp.int32(16))
    return jnp.concatenate([low, high], axis=0)


def encode_scores(x):
    step = jnp.full_like(x, 65536.0)
    octave = jnp.full(x.shape, -8192, I32)
    edge, scale = 0.25, 32768.0
    for level in range(7):
        above = x >= edge
        step = jnp.where(above, scale, step)
        octave = jnp.where(above, level * 8192, octave)
        edge, scale = edge * 2.0, scale * 0.5
    return (x * step).astype(I32) + octave


def decode_scores(codes):
    octave = lax.shift_right_logical(codes, jnp.int32(13))
    mantissa = lax.bitwise_and(codes, jnp.int32(8191)).astype(F32) + 8192.5
    power = lax.shift_left(jnp.full_like(codes, 1), octave).astype(F32)
    return mantissa * (power * (1.0 / 65536.0))


def kernel(
    N, C, NB, CAP, RT,
    scores, prior, tiles, info, out,
    words, rx_words, pwords, rx_pwords, owords, rx_owords,
    all_tiles, field, low, votes, rx_info, sm,
    sums, rx_sums, csums, rx_csums, total, side, rx_side, osum, rx_osum, mine,
    local_sem, sm_sem,
    info_s, info_r, tz_s, tz_r, tx_s, tx_r, tc_s, tc_r, td_s, td_r,
    sc_s, sc_r, pr_s, pr_r, c1_s, c1_r, z1_s, z1_r, sd_s, sd_r, o_s, o_r, c2_s, c2_r,
):
    n = lax.axis_index("nodes")
    c = lax.axis_index("classes")
    SL = N * CAP
    HR = RT // 2

    def znode(k):
        return lax.rem(n + k, N)

    def zfrom(k):
        return lax.rem(n - k + N, N)

    def cnode(k):
        return lax.rem(c + k, C)

    def cfrom(k):
        return lax.rem(c - k + C, C)

    xpeer = lax.rem(c + 2, C)
    kpeer = c + 1 - 2 * lax.rem(c, 2)
    xkpeer = lax.rem(kpeer + 2, C)
    order = [2, 1, 3]

    def remote(src, dst, s, r, **to):
        return pltpu.make_async_remote_copy(
            src_ref=src, dst_ref=dst, send_sem=s, recv_sem=r, device_id=to, device_id_type=MESH
        )

    barrier = pltpu.get_barrier_semaphore()
    for k in range(1, N):
        pl.semaphore_signal(barrier, inc=1, device_id={"nodes": znode(k)}, device_id_type=MESH)
    for k in range(1, C):
        pl.semaphore_signal(barrier, inc=1, device_id={"classes": cnode(k)}, device_id_type=MESH)

    own_tiles = pltpu.make_async_copy(tiles, all_tiles.at[n], local_sem)
    own_tiles.start()
    rx_info[n] = info[...]

    def code_scores(d, carry):
        rows = pl.ds(pl.multiple_of(d * RT, RT), RT)
        for b in range(NB):
            words[d, b] = pack(encode_scores(scores[rows, b * 128:(b + 1) * 128]))
        return carry

    lax.fori_loop(0, N, code_scores, 0)
    pl.semaphore_wait(barrier, N - 1 + C - 1)

    infos = [remote(info, rx_info.at[n], info_s.at[k], info_r.at[k], nodes=znode(k)) for k in order]
    tzs = [
        remote(tiles.at[c], all_tiles.at[n, c], tz_s.at[k], tz_r.at[k], nodes=znode(k))
        for k in order
    ]
    scs = [
        remote(words.at[znode(k)], rx_words.at[n], sc_s.at[k], sc_r.at[k], nodes=znode(k))
        for k in order
    ]
    for copy in infos + tzs + scs:
        copy.start()

    def code_prior(d, carry):
        rows = pl.ds(pl.multiple_of(d * RT, RT), RT)
        for b in range(NB):
            pwords[d, b] = pack(
                (prior[rows, b * 128:(b + 1) * 128] * 32767.5 + 0.5).astype(I32)
            )
        return carry

    lax.fori_loop(0, N, code_prior, 0)
    prs = [
        remote(pwords.at[znode(k)], rx_pwords.at[n], pr_s.at[k], pr_r.at[k], nodes=znode(k))
        for k in order
    ]
    for copy in prs:
        copy.start()

    own_rows = pl.ds(pl.multiple_of(n * RT, RT), RT)
    for b in range(NB):
        x = scores[own_rows, b * 128:(b + 1) * 128]
        field[n * NB + b] = x
        low[n * NB + b] = x.astype(jnp.bfloat16)
    rx_pwords[n] = pwords[n]

    waiting = [1, 3, 2]
    txs, tcs, tds = [], [], []
    for k in waiting:
        p = zfrom(k)
        remote(tiles.at[c], all_tiles.at[p, c], tz_s.at[k], tz_r.at[k], nodes=p).wait_recv()
        txs.append(
            remote(all_tiles.at[p, c], all_tiles.at[p, c], tx_s.at[k], tx_r.at[k], classes=xpeer)
        )
        tcs.append(
            remote(all_tiles.at[p, c], all_tiles.at[p, c], tc_s.at[k], tc_r.at[k], classes=kpeer)
        )
        txs[-1].start()
        tcs[-1].start()
    for k in order:
        remote(info, rx_info.at[zfrom(k)], info_s.at[k], info_r.at[k], nodes=zfrom(k)).wait_recv()
    to_sm = pltpu.make_async_copy(rx_info.at[:, 0:8], sm, sm_sem)
    to_sm.start()
    for k in waiting:
        p = zfrom(k)
        remote(words.at[p], rx_words.at[p], sc_s.at[k], sc_r.at[k], nodes=p).wait_recv()

        def take_scores(b, carry):
            x = decode_scores(unpack(rx_words[p, b]))
            field[p * NB + b] = x
            low[p * NB + b] = x.astype(jnp.bfloat16)
            return carry

        lax.fori_loop(0, NB, take_scores, 0)
    to_sm.wait()
    own_tiles.wait()
    for k in waiting:
        p = zfrom(k)
        remote(
            all_tiles.at[p, xpeer], all_tiles.at[p, xpeer], tx_s.at[k], tx_r.at[k], classes=xpeer
        ).wait_recv()
        tds.append(
            remote(
                all_tiles.at[p, xpeer], all_tiles.at[p, xpeer], td_s.at[k], td_r.at[k], classes=kpeer
            )
        )
        tds[-1].start()
    for k in waiting:
        p = zfrom(k)
        remote(
            all_tiles.at[p, kpeer], all_tiles.at[p, kpeer], tc_s.at[k], tc_r.at[k], classes=kpeer
        ).wait_recv()
        remote(
            all_tiles.at[p, xkpeer], all_tiles.at[p, xkpeer], td_s.at[k], td_r.at[k], classes=kpeer
        ).wait_recv()

    def cast_votes(d):
        def one(p, carry):
            for s in range(CAP):
                col = sm[p, 0, d * CAP + s]
                block = jnp.dot(
                    low[p * NB + col], all_tiles[p, d, s], preferred_element_type=F32
                )
                votes[p * CAP + s] = block.astype(jnp.bfloat16).astype(F32)
            return carry

        lax.fori_loop(0, N, one, 0)

    def tally(d, b):
        acc = field[d * NB + b]
        for i in range(SL):
            p, s = i // CAP, i % CAP
            row = sm[d, 0, SL + i]
            hit = jnp.logical_and(row == b, s < sm[d, 0, 2 * SL + p])
            acc = acc + jnp.where(hit, 1.0, 0.0).astype(F32) * votes[i]
        return acc

    def first(d, carry):
        cast_votes(d)

        def one(b, carry):
            acc = tally(d, b)
            field[d * NB + b] = acc
            sums[d, pl.ds(b, 1)] = jnp.sum(acc, axis=0, keepdims=True)
            return carry

        lax.fori_loop(0, NB, one, 0)
        return carry

    lax.fori_loop(0, N, first, 0)

    rx_sums[c] = sums[...]
    c1s = [remote(sums, rx_sums.at[c], c1_s.at[k], c1_r.at[k], classes=cnode(k)) for k in range(1, C)]
    for copy in c1s:
        copy.start()
    for k in range(1, C):
        p = cfrom(k)
        remote(sums, rx_sums.at[p], c1_s.at[k], c1_r.at[k], classes=p).wait_recv()
    whole = rx_sums[0]
    for k in range(1, C):
        whole = whole + rx_sums[k]
    csums[...] = whole
    rx_csums[n] = whole
    z1s = [remote(csums, rx_csums.at[n], z1_s.at[k], z1_r.at[k], nodes=znode(k)) for k in order]
    for copy in z1s:
        copy.start()
    for k in waiting:
        p = zfrom(k)
        remote(csums, rx_csums.at[p], z1_s.at[k], z1_r.at[k], nodes=p).wait_recv()
    whole = rx_csums[0]
    for k in range(1, N):
        whole = whole + rx_csums[k]
    total[...] = 1024.0 / whole

    def spread(p):
        def one(b, carry):
            seeded = 0.5 * rx_info[p, pl.ds(8 + b, 1)].astype(F32)
            normed = field[p * NB + b] * total[p, pl.ds(b, 1)]
            seeds = unpack(rx_pwords[p, b]).astype(F32) * (1.0 / 32767.5)
            x = normed + seeded * (seeds - normed)
            field[p * NB + b] = x
            low[p * NB + b] = x.astype(jnp.bfloat16)
            return carry

        lax.fori_loop(0, NB, one, 0)

    spread(n)
    for k in waiting:
        p = zfrom(k)
        remote(pwords.at[p], rx_pwords.at[p], pr_s.at[k], pr_r.at[k], nodes=p).wait_recv()
        spread(p)

    sds, outs = [], []
    for k in order:
        d = znode(k)
        cast_votes(d)

        def one(b, carry):
            acc = tally(d, b)
            side[d, pl.ds(b, 1)] = jnp.sum(acc, axis=0, keepdims=True)
            peak = jnp.maximum(jnp.max(acc, axis=0, keepdims=True), 1e-30)
            side[d, pl.ds(8 + b, 1)] = peak * (1.0 / 65535.0)
            owords[d, b] = pack((acc * (65535.0 / peak) + 0.5).astype(I32))
            return carry

        lax.fori_loop(0, NB, one, 0)
        sds.append(remote(side.at[d], rx_side.at[n], sd_s.at[k], sd_r.at[k], nodes=d))
        outs.append(remote(owords.at[d], rx_owords.at[n], o_s.at[k], o_r.at[k], nodes=d))
        sds[-1].start()
        outs[-1].start()
    cast_votes(n)

    def own(b, carry):
        acc = tally(n, b)
        mine[b] = acc
        rx_side[n, pl.ds(b, 1)] = jnp.sum(acc, axis=0, keepdims=True)
        return carry

    lax.fori_loop(0, NB, own, 0)

    for k in waiting:
        p = zfrom(k)
        remote(side.at[p], rx_side.at[p], sd_s.at[k], sd_r.at[k], nodes=p).wait_recv()
    whole = rx_side[0, 0:8]
    for p in range(1, N):
        whole = whole + rx_side[p, 0:8]
    osum[...] = whole
    rx_osum[c] = whole
    c2s = [remote(osum, rx_osum.at[c], c2_s.at[k], c2_r.at[k], classes=cnode(k)) for k in range(1, C)]
    for copy in c2s:
        copy.start()
    for k in range(1, C):
        p = cfrom(k)
        remote(osum, rx_osum.at[p], c2_s.at[k], c2_r.at[k], classes=p).wait_recv()
    whole = rx_osum[0]
    for k in range(1, C):
        whole = whole + rx_osum[k]
    total[n] = 1024.0 / whole

    def finish(p, b, tallied):
        seeded = 0.5 * info[8 + b:9 + b].astype(F32)
        rows = pl.ds(pl.multiple_of(p * RT, RT), RT)
        normed = tallied * total[n, b:b + 1]
        out[rows, b * 128:(b + 1) * 128] = normed + seeded * (
            prior[rows, b * 128:(b + 1) * 128] - normed
        )

    for b in range(NB):
        finish(n, b, mine[b])
    for k in waiting:
        p = zfrom(k)
        remote(owords.at[p], rx_owords.at[p], o_s.at[k], o_r.at[k], nodes=p).wait_recv()
        for b in range(NB):
            codes = unpack(rx_owords[p, b]).astype(F32)
            finish(p, b, codes * rx_side[p, 8 + b:9 + b])

    for copy in infos + tzs + scs + prs + txs + tcs + tds + c1s + z1s + sds + outs + c2s:
        copy.wait_send()


def fits(mesh, scores, tiles):
    return (
        mesh.shape["nodes"] == 4
        and mesh.shape["classes"] == 4
        and scores.shape[1] // tiles.shape[-1] == 8
        and tiles.shape[-1] == 128
        and (scores.shape[0] // 4) % 16 == 0
        and 2 * tiles.shape[1] * tiles.shape[2] + tiles.shape[1] <= 128
    )


def transposed(N, C, scores, prior, tiles, col_tile, row_tile, counts, seed_mask):
    R = scores.shape[0]
    CAP = tiles.shape[2]
    TW = tiles.shape[-1]
    NB = scores.shape[1] // TW
    RT = R // N
    SL = N * CAP
    line = jnp.concatenate(
        [col_tile[0].reshape(-1), row_tile[:, 0].reshape(-1), counts[:, 0]]
    )
    line = jnp.pad(line, (0, 8 * TW - line.shape[0])).reshape(8, TW)
    info = jnp.concatenate([line, seed_mask.reshape(NB, TW)], axis=0)
    V = pltpu.VMEM
    words = V((N, NB, RT // 2, TW), I32)
    dma = pltpu.SemaphoreType.DMA
    pairs = [dma((4,)) for _ in range(24)]
    vm = pl.BlockSpec(memory_space=pltpu.VMEM)
    return pl.pallas_call(
        functools.partial(kernel, N, C, NB, CAP, RT),
        out_shape=jax.ShapeDtypeStruct(scores.shape, F32),
        in_specs=[vm] * 4,
        out_specs=vm,
        scratch_shapes=[
            words, words, words, words, words, words,
            V((N, N, CAP, TW, TW), jnp.bfloat16),
            V((N * NB, RT, TW), F32),
            V((N * NB, RT, TW), jnp.bfloat16),
            V((SL, RT, TW), F32),
            V((N, 16, TW), I32),
            pltpu.SMEM((N, 8, TW), I32),
            V((N, NB, TW), F32),
            V((C, N, NB, TW), F32),
            V((N, NB, TW), F32),
            V((N, N, NB, TW), F32),
            V((N, NB, TW), F32),
            V((N, 16, TW), F32),
            V((N, 16, TW), F32),
            V((NB, TW), F32),
            V((C, NB, TW), F32),
            V((NB, RT, TW), F32),
            dma,
            dma,
            *pairs,
        ],
        compiler_params=pltpu.CompilerParams(
            collective_id=0, has_side_effects=True, vmem_limit_bytes=40 * 1024 * 1024
        ),
    )(scores, prior, tiles[0], info)


def solution(mesh):
    placed = (
        P("classes", ("groups", "nodes")),
        P("classes", ("groups", "nodes")),
        P(("groups", "nodes"), None, None, None, None),
        P(("groups", "nodes"), None, None),
        P("groups", "nodes", None),
        P("groups", "nodes"),
        P(("groups", "nodes")),
    )

    def one_device(scores, prior, tiles, *rest):
        if fits(mesh, scores, tiles):
            return transposed(
                mesh.shape["nodes"], mesh.shape["classes"], scores, prior, tiles, *rest
            )
        return body(scores, prior, tiles, *rest)

    return jax.shard_map(
        one_device,
        mesh=mesh,
        in_specs=placed,
        out_specs=P("classes", ("groups", "nodes")),
        check_vma=False,
    )
```

```python
import functools

import jax
import jax.numpy as jnp
from jax import lax
from jax.experimental import pallas as pl
from jax.experimental.pallas import tpu as pltpu
from jax.sharding import PartitionSpec as P

CLASSES = 1024
ITERS = 2
MESH = pl.DeviceIdType.MESH
PIECES = 3
LAG = 3
FIRST = 3
F32 = jnp.float32
I32 = jnp.int32


def body(scores, prior, tiles, col_tile, row_tile, counts, seed_mask):
    tiles = tiles[0]
    col_tile = col_tile[0]
    incoming_rows = row_tile[:, 0]
    incoming_counts = counts[:, 0]
    tile_width = tiles.shape[-1]
    class_rows = scores.shape[0]
    block_count = scores.shape[1] // tile_width
    usable = lax.broadcasted_iota(jnp.int32, incoming_rows.shape, 1) < incoming_counts[:, None]
    target_pick = jax.nn.one_hot(incoming_rows, block_count, dtype=jnp.bfloat16) * usable[
        ..., None
    ].astype(jnp.bfloat16)
    source_pick = jax.nn.one_hot(col_tile, block_count, dtype=jnp.bfloat16)
    seeded = seed_mask.astype(jnp.float32)[None, :]
    scores_now = scores
    for sweep in range(ITERS):
        field_low = scores_now.astype(jnp.bfloat16).reshape(class_rows, block_count, tile_width)
        picked = jnp.einsum(
            "pse,cek->psck", source_pick, field_low, preferred_element_type=jnp.float32
        ).astype(jnp.bfloat16)
        products = jnp.einsum(
            "psck,pskj->pscj", picked, tiles, preferred_element_type=jnp.float32
        ).astype(jnp.bfloat16)
        arrived = lax.all_to_all(products, "nodes", split_axis=0, concat_axis=0, tiled=True)
        gathered = jnp.einsum(
            "pse,pscj->cej", target_pick, arrived, preferred_element_type=jnp.float32
        )
        tallied = scores_now + gathered.reshape(class_rows, block_count * tile_width)
        node_total = lax.psum(jnp.sum(tallied, axis=0), "classes")
        normed = CLASSES * tallied / node_total[None, :]
        scores_now = normed + 0.5 * seeded * (prior - normed)
    return scores_now


def pack(codes):
    half = codes.shape[0] // 2
    return lax.bitwise_or(codes[:half], lax.shift_left(codes[half:], jnp.int32(16)))


def unpack(words):
    low = lax.bitwise_and(words, jnp.int32(0xFFFF))
    high = lax.shift_right_logical(words, jnp.int32(16))
    return jnp.concatenate([low, high], axis=0)


def encode_scores(x):
    step = jnp.full_like(x, 65536.0)
    octave = jnp.full(x.shape, -8192, I32)
    edge, scale = 0.25, 32768.0
    for level in range(7):
        above = x >= edge
        step = jnp.where(above, scale, step)
        octave = jnp.where(above, level * 8192, octave)
        edge, scale = edge * 2.0, scale * 0.5
    return (x * step).astype(I32) + octave


def decode_scores(codes):
    octave = lax.shift_right_logical(codes, jnp.int32(13))
    mantissa = lax.bitwise_and(codes, jnp.int32(8191)).astype(F32) + 8192.5
    power = lax.shift_left(jnp.full_like(codes, 1), octave).astype(F32)
    return mantissa * (power * (1.0 / 65536.0))


def kernel(
    N, C, NB, CAP, RT,
    scores_in, prior_in, tiles, col_tile, row_tile, counts, seeds_in, out,
    scores, prior, info,
    words, rx_words, pwords, rx_pwords, owords, rx_owords,
    all_tiles, field, low, votes, rx_info, sm,
    sums, rx_sums, csums, rx_csums, total, side, rx_side, osum, rx_osum, mine,
    local_sem, scores_sem, prior_sem, sm_sem,
    info_s, info_r, tz_s, tz_r, tx_s, tx_r, tc_s, tc_r, td_s, td_r,
    sc_s, sc_r, pr_s, pr_r, c1_s, c1_r, z1_s, z1_r, sd_s, sd_r, o_s, o_r, c2_s, c2_r,
):
    n = lax.axis_index("nodes")
    c = lax.axis_index("classes")
    SL = N * CAP
    HR = RT // 2

    def znode(k):
        return lax.rem(n + k, N)

    def zfrom(k):
        return lax.rem(n - k + N, N)

    def cnode(k):
        return lax.rem(c + k, C)

    def cfrom(k):
        return lax.rem(c - k + C, C)

    xpeer = lax.rem(c + 2, C)
    kpeer = c + 1 - 2 * lax.rem(c, 2)
    xkpeer = lax.rem(kpeer + 2, C)
    order = [2, 1, 3]
    waiting = [1, 3, 2]
    PIECE = CAP // PIECES

    def remote(src, dst, s, r, **to):
        return pltpu.make_async_remote_copy(
            src_ref=src, dst_ref=dst, send_sem=s, recv_sem=r, device_id=to, device_id_type=MESH
        )

    barrier = pltpu.get_barrier_semaphore()
    for k in range(1, N):
        pl.semaphore_signal(barrier, inc=1, device_id={"nodes": znode(k)}, device_id_type=MESH)
    for k in range(1, C):
        pl.semaphore_signal(barrier, inc=1, device_id={"classes": cnode(k)}, device_id_type=MESH)

    load_scores = pltpu.make_async_copy(scores_in, scores, scores_sem)
    load_scores.start()
    own_tiles = pltpu.make_async_copy(tiles, all_tiles.at[n], local_sem)
    own_tiles.start()
    load_prior = pltpu.make_async_copy(prior_in, prior, prior_sem)
    load_prior.start()

    lane = lax.broadcasted_iota(I32, (8, 128), 1)
    line = jnp.zeros((8, 128), I32)
    for d in range(N):
        for s in range(CAP):
            line = jnp.where(lane == d * CAP + s, col_tile[0, d, s], line)
            line = jnp.where(lane == SL + d * CAP + s, row_tile[d, 0, s], line)
        line = jnp.where(lane == 2 * SL + d, counts[d], line)
    info[0:8] = line
    info[8:16] = seeds_in[...]
    rx_info[n] = info[...]

    pieces = [(h, k) for h in range(PIECES) for k in waiting]

    def piece(p, q, h):
        return all_tiles.at[p, q, pl.ds(h * PIECE, PIECE)]

    def tile_z(h, k):
        i = h * N + k
        return remote(
            tiles.at[c, pl.ds(h * PIECE, PIECE)], piece(n, c, h), tz_s.at[i], tz_r.at[i], nodes=znode(k)
        )

    def tile_x(h, k):
        i = h * N + k
        here = piece(zfrom(k), c, h)
        return remote(here, here, tx_s.at[i], tx_r.at[i], classes=xpeer)

    def tile_c(h, k):
        i = h * N + k
        here = piece(zfrom(k), c, h)
        return remote(here, here, tc_s.at[i], tc_r.at[i], classes=kpeer)

    def tile_d(h, k):
        i = h * N + k
        here = piece(zfrom(k), xpeer, h)
        return remote(here, here, td_s.at[i], td_r.at[i], classes=kpeer)

    pl.semaphore_wait(barrier, N - 1 + C - 1)
    infos = [remote(info, rx_info.at[n], info_s.at[k], info_r.at[k], nodes=znode(k)) for k in order]
    tzs = [tile_z(h, k) for h, k in pieces]
    for copy in infos + tzs[:FIRST]:
        copy.start()

    load_scores.wait()
    scs = []
    for k in order:
        d = znode(k)

        def code_scores(b, carry):
            rows = pl.ds(pl.multiple_of(d * RT, RT), RT)
            cols = pl.ds(pl.multiple_of(b * 128, 128), 128)
            words[d, b] = pack(encode_scores(scores[rows, cols]))
            return carry

        lax.fori_loop(0, NB, code_scores, 0)
        scs.append(remote(words.at[d], rx_words.at[n], sc_s.at[k], sc_r.at[k], nodes=d))
        scs[-1].start()
    for copy in tzs[FIRST:]:
        copy.start()

    own_rows = pl.ds(pl.multiple_of(n * RT, RT), RT)
    for b in range(NB):
        x = scores[own_rows, b * 128:(b + 1) * 128]
        field[n * NB + b] = x
        low[n * NB + b] = x.astype(jnp.bfloat16)

    def code_prior(d, carry):
        rows = pl.ds(pl.multiple_of(d * RT, RT), RT)
        for b in range(NB):
            pwords[d, b] = pack(
                (prior[rows, b * 128:(b + 1) * 128] * 32767.5 + 0.5).astype(I32)
            )
        return carry

    load_prior.wait()
    lax.fori_loop(0, N, code_prior, 0)
    rx_pwords[n] = pwords[n]

    txs, tcs, tds = [], [], []

    def relay_x(h, k):
        i = h * N + k
        here = piece(zfrom(k), xpeer, h)
        remote(here, here, tx_s.at[i], tx_r.at[i], classes=xpeer).wait_recv()
        tds.append(tile_d(h, k))
        tds[-1].start()

    for i, (h, k) in enumerate(pieces):
        j = h * N + k
        here = piece(zfrom(k), c, h)
        remote(here, here, tz_s.at[j], tz_r.at[j], nodes=zfrom(k)).wait_recv()
        txs.append(tile_x(h, k))
        txs[-1].start()
        tcs.append(tile_c(h, k))
        tcs[-1].start()
        if i >= LAG:
            relay_x(*pieces[i - LAG])
    prs = [
        remote(pwords.at[znode(k)], rx_pwords.at[n], pr_s.at[k], pr_r.at[k], nodes=znode(k))
        for k in order
    ]
    for copy in prs:
        copy.start()
    for h, k in pieces[-LAG:]:
        relay_x(h, k)
    for k in order:
        remote(info, rx_info.at[zfrom(k)], info_s.at[k], info_r.at[k], nodes=zfrom(k)).wait_recv()
    to_sm = pltpu.make_async_copy(rx_info.at[:, 0:8], sm, sm_sem)
    to_sm.start()
    for k in waiting:
        p = zfrom(k)
        remote(words.at[p], rx_words.at[p], sc_s.at[k], sc_r.at[k], nodes=p).wait_recv()

        def take_scores(b, carry):
            x = decode_scores(unpack(rx_words[p, b]))
            field[p * NB + b] = x
            low[p * NB + b] = x.astype(jnp.bfloat16)
            return carry

        lax.fori_loop(0, NB, take_scores, 0)
    to_sm.wait()
    own_tiles.wait()

    def cast(p, d):
        for s in range(CAP):
            col = sm[p, 0, d * CAP + s]
            block = jnp.dot(low[p * NB + col], all_tiles[p, d, s], preferred_element_type=F32)
            votes[d * SL + p * CAP + s] = block.astype(jnp.bfloat16).astype(F32)

    def cast_from(p):
        lax.fori_loop(0, N, lambda d, carry: (cast(p, d), carry)[1], 0)

    def cast_votes(d):
        lax.fori_loop(0, N, lambda p, carry: (cast(p, d), carry)[1], 0)

    def tally(d, b):
        acc = field[d * NB + b]
        for i in range(SL):
            p, s = i // CAP, i % CAP
            row = sm[d, 0, SL + i]
            hit = jnp.logical_and(row == b, s < sm[d, 0, 2 * SL + p])
            acc = acc + jnp.where(hit, 1.0, 0.0).astype(F32) * votes[d * SL + i]
        return acc

    cast_from(n)
    for k in waiting:
        for h in range(PIECES):
            i = h * N + k
            here = piece(zfrom(k), kpeer, h)
            remote(here, here, tc_s.at[i], tc_r.at[i], classes=kpeer).wait_recv()
            here = piece(zfrom(k), xkpeer, h)
            remote(here, here, td_s.at[i], td_r.at[i], classes=kpeer).wait_recv()
        cast_from(zfrom(k))

    def first(d, carry):
        def one(b, carry):
            acc = tally(d, b)
            field[d * NB + b] = acc
            sums[d, pl.ds(b, 1)] = jnp.sum(acc, axis=0, keepdims=True)
            return carry

        lax.fori_loop(0, NB, one, 0)
        return carry

    lax.fori_loop(0, N, first, 0)

    rx_sums[c] = sums[...]
    c1s = [remote(sums, rx_sums.at[c], c1_s.at[k], c1_r.at[k], classes=cnode(k)) for k in range(1, C)]
    for copy in c1s:
        copy.start()
    for k in range(1, C):
        p = cfrom(k)
        remote(sums, rx_sums.at[p], c1_s.at[k], c1_r.at[k], classes=p).wait_recv()
    whole = rx_sums[0]
    for k in range(1, C):
        whole = whole + rx_sums[k]
    csums[...] = whole
    rx_csums[n] = whole
    z1s = [remote(csums, rx_csums.at[n], z1_s.at[k], z1_r.at[k], nodes=znode(k)) for k in order]
    for copy in z1s:
        copy.start()
    for k in waiting:
        p = zfrom(k)
        remote(csums, rx_csums.at[p], z1_s.at[k], z1_r.at[k], nodes=p).wait_recv()
    whole = rx_csums[0]
    for k in range(1, N):
        whole = whole + rx_csums[k]
    total[...] = 1024.0 / whole

    def spread(p):
        def one(b, carry):
            seeded = 0.5 * rx_info[p, pl.ds(8 + b, 1)].astype(F32)
            normed = field[p * NB + b] * total[p, pl.ds(b, 1)]
            seeds = unpack(rx_pwords[p, b]).astype(F32) * (1.0 / 32767.5)
            x = normed + seeded * (seeds - normed)
            field[p * NB + b] = x
            low[p * NB + b] = x.astype(jnp.bfloat16)
            return carry

        lax.fori_loop(0, NB, one, 0)

    spread(n)
    for k in waiting:
        p = zfrom(k)
        remote(pwords.at[p], rx_pwords.at[p], pr_s.at[k], pr_r.at[k], nodes=p).wait_recv()
        spread(p)

    sds, outs = [], []
    for k in order:
        d = znode(k)
        cast_votes(d)

        def one(b, carry):
            acc = tally(d, b)
            side[d, pl.ds(b, 1)] = jnp.sum(acc, axis=0, keepdims=True)
            peak = jnp.maximum(jnp.max(acc, axis=0, keepdims=True), 1e-30)
            side[d, pl.ds(8 + b, 1)] = peak * (1.0 / 65535.0)
            owords[d, b] = pack((acc * (65535.0 / peak) + 0.5).astype(I32))
            return carry

        lax.fori_loop(0, NB, one, 0)
        sds.append(remote(side.at[d], rx_side.at[n], sd_s.at[k], sd_r.at[k], nodes=d))
        outs.append(remote(owords.at[d], rx_owords.at[n], o_s.at[k], o_r.at[k], nodes=d))
        sds[-1].start()
        outs[-1].start()
    cast_votes(n)

    def own(b, carry):
        acc = tally(n, b)
        mine[b] = acc
        rx_side[n, pl.ds(b, 1)] = jnp.sum(acc, axis=0, keepdims=True)
        return carry

    lax.fori_loop(0, NB, own, 0)

    for k in waiting:
        p = zfrom(k)
        remote(side.at[p], rx_side.at[p], sd_s.at[k], sd_r.at[k], nodes=p).wait_recv()
    whole = rx_side[0, 0:8]
    for p in range(1, N):
        whole = whole + rx_side[p, 0:8]
    osum[...] = whole
    rx_osum[c] = whole
    c2s = [remote(osum, rx_osum.at[c], c2_s.at[k], c2_r.at[k], classes=cnode(k)) for k in range(1, C)]
    for copy in c2s:
        copy.start()
    for k in range(1, C):
        p = cfrom(k)
        remote(osum, rx_osum.at[p], c2_s.at[k], c2_r.at[k], classes=p).wait_recv()
    whole = rx_osum[0]
    for k in range(1, C):
        whole = whole + rx_osum[k]
    total[n] = 1024.0 / whole

    def finish(p, b, tallied):
        seeded = 0.5 * info[8 + b:9 + b].astype(F32)
        rows = pl.ds(pl.multiple_of(p * RT, RT), RT)
        normed = tallied * total[n, b:b + 1]
        out[rows, b * 128:(b + 1) * 128] = normed + seeded * (
            prior[rows, b * 128:(b + 1) * 128] - normed
        )

    for b in range(NB):
        finish(n, b, mine[b])
    for k in waiting:
        p = zfrom(k)
        remote(owords.at[p], rx_owords.at[p], o_s.at[k], o_r.at[k], nodes=p).wait_recv()
        for b in range(NB):
            codes = unpack(rx_owords[p, b]).astype(F32)
            finish(p, b, codes * rx_side[p, 8 + b:9 + b])

    for copy in infos + tzs + scs + prs + txs + tcs + tds + c1s + z1s + sds + outs + c2s:
        copy.wait_send()


def fits(mesh, scores, tiles):
    return (
        mesh.shape["nodes"] == 4
        and mesh.shape["classes"] == 4
        and scores.shape[1] // tiles.shape[-1] == 8
        and tiles.shape[-1] == 128
        and (scores.shape[0] // 4) % 16 == 0
        and tiles.shape[2] % PIECES == 0
        and 2 * tiles.shape[1] * tiles.shape[2] + tiles.shape[1] <= 128
    )


def transposed(N, C, scores, prior, tiles, col_tile, row_tile, counts, seed_mask):
    R = scores.shape[0]
    CAP = tiles.shape[2]
    TW = tiles.shape[-1]
    NB = scores.shape[1] // TW
    RT = R // N
    SL = N * CAP
    V = pltpu.VMEM
    words = V((N, NB, RT // 2, TW), I32)
    dma = pltpu.SemaphoreType.DMA
    sems = [4] * 2 + [4 * PIECES] * 8 + [4] * 14
    pairs = [dma((size,)) for size in sems]
    smem = pl.BlockSpec(memory_space=pltpu.SMEM)
    anywhere = pl.BlockSpec(memory_space=pl.ANY)
    vm = pl.BlockSpec(memory_space=pltpu.VMEM)
    return pl.pallas_call(
        functools.partial(kernel, N, C, NB, CAP, RT),
        out_shape=jax.ShapeDtypeStruct(scores.shape, F32),
        in_specs=[anywhere] * 3 + [smem] * 3 + [vm],
        out_specs=vm,
        scratch_shapes=[
            V(scores.shape, F32), V(scores.shape, F32), V((16, TW), I32),
            words, words, words, words, words, words,
            V((N, N, CAP, TW, TW), jnp.bfloat16),
            V((N * NB, RT, TW), F32),
            V((N * NB, RT, TW), jnp.bfloat16),
            V((N * SL, RT, TW), F32),
            V((N, 16, TW), I32),
            pltpu.SMEM((N, 8, TW), I32),
            V((N, NB, TW), F32),
            V((C, N, NB, TW), F32),
            V((N, NB, TW), F32),
            V((N, N, NB, TW), F32),
            V((N, NB, TW), F32),
            V((N, 16, TW), F32),
            V((N, 16, TW), F32),
            V((NB, TW), F32),
            V((C, NB, TW), F32),
            V((NB, RT, TW), F32),
            dma, dma, dma, dma,
            *pairs,
        ],
        compiler_params=pltpu.CompilerParams(
            collective_id=0, has_side_effects=True, vmem_limit_bytes=60 * 1024 * 1024
        ),
    )(scores, prior, tiles[0], col_tile, row_tile, counts[:, 0], seed_mask.reshape(NB, TW))


def solution(mesh):
    placed = (
        P("classes", ("groups", "nodes")),
        P("classes", ("groups", "nodes")),
        P(("groups", "nodes"), None, None, None, None),
        P(("groups", "nodes"), None, None),
        P("groups", "nodes", None),
        P("groups", "nodes"),
        P(("groups", "nodes")),
    )

    def one_device(scores, prior, tiles, *rest):
        if fits(mesh, scores, tiles):
            return transposed(
                mesh.shape["nodes"], mesh.shape["classes"], scores, prior, tiles, *rest
            )
        return body(scores, prior, tiles, *rest)

    return jax.shard_map(
        one_device,
        mesh=mesh,
        in_specs=placed,
        out_specs=P("classes", ("groups", "nodes")),
        check_vma=False,
    )
```

```python
import functools

import jax
import jax.numpy as jnp
from jax import lax
from jax.experimental import pallas as pl
from jax.experimental.pallas import tpu as pltpu
from jax.sharding import PartitionSpec as P

CLASSES = 1024
ITERS = 2
MESH = pl.DeviceIdType.MESH
PIECES = 3
LAG = 3
F32 = jnp.float32
I32 = jnp.int32


def body(scores, prior, tiles, col_tile, row_tile, counts, seed_mask):
    tiles = tiles[0]
    col_tile = col_tile[0]
    incoming_rows = row_tile[:, 0]
    incoming_counts = counts[:, 0]
    tile_width = tiles.shape[-1]
    class_rows = scores.shape[0]
    block_count = scores.shape[1] // tile_width
    usable = lax.broadcasted_iota(jnp.int32, incoming_rows.shape, 1) < incoming_counts[:, None]
    target_pick = jax.nn.one_hot(incoming_rows, block_count, dtype=jnp.bfloat16) * usable[
        ..., None
    ].astype(jnp.bfloat16)
    source_pick = jax.nn.one_hot(col_tile, block_count, dtype=jnp.bfloat16)
    seeded = seed_mask.astype(jnp.float32)[None, :]
    scores_now = scores
    for sweep in range(ITERS):
        field_low = scores_now.astype(jnp.bfloat16).reshape(class_rows, block_count, tile_width)
        picked = jnp.einsum(
            "pse,cek->psck", source_pick, field_low, preferred_element_type=jnp.float32
        ).astype(jnp.bfloat16)
        products = jnp.einsum(
            "psck,pskj->pscj", picked, tiles, preferred_element_type=jnp.float32
        ).astype(jnp.bfloat16)
        arrived = lax.all_to_all(products, "nodes", split_axis=0, concat_axis=0, tiled=True)
        gathered = jnp.einsum(
            "pse,pscj->cej", target_pick, arrived, preferred_element_type=jnp.float32
        )
        tallied = scores_now + gathered.reshape(class_rows, block_count * tile_width)
        node_total = lax.psum(jnp.sum(tallied, axis=0), "classes")
        normed = CLASSES * tallied / node_total[None, :]
        scores_now = normed + 0.5 * seeded * (prior - normed)
    return scores_now


def pack(codes):
    half = codes.shape[0] // 2
    return lax.bitwise_or(codes[:half], lax.shift_left(codes[half:], jnp.int32(16)))


def unpack(words):
    low = lax.bitwise_and(words, jnp.int32(0xFFFF))
    high = lax.shift_right_logical(words, jnp.int32(16))
    return jnp.concatenate([low, high], axis=0)


def encode_scores(x):
    step = jnp.full_like(x, 65536.0)
    octave = jnp.full(x.shape, -8192, I32)
    edge, scale = 0.25, 32768.0
    for level in range(7):
        above = x >= edge
        step = jnp.where(above, scale, step)
        octave = jnp.where(above, level * 8192, octave)
        edge, scale = edge * 2.0, scale * 0.5
    return (x * step).astype(I32) + octave


def decode_scores(codes):
    octave = lax.shift_right_logical(codes, jnp.int32(13))
    mantissa = lax.bitwise_and(codes, jnp.int32(8191)).astype(F32) + 8192.5
    power = lax.shift_left(jnp.full_like(codes, 1), octave).astype(F32)
    return mantissa * (power * (1.0 / 65536.0))


def kernel(
    N, C, NB, CAP, RT,
    scores_in, prior_in, tiles, col_tile, row_tile, counts, seeds_in, out,
    scores, prior, info,
    words, rx_words, pwords, rx_pwords, owords, rx_owords,
    all_tiles, field, low, votes, rx_info, sm,
    sums, rx_sums, csums, rx_csums, total, side, rx_side, osum, rx_osum, mine,
    local_sem, scores_sem, prior_sem, sm_sem,
    info_s, info_r, tz_s, tz_r, tf_s, tx_s, tx_r, tc_s, tc_r, td_s, td_r,
    sc_s, sc_r, pr_s, pr_r, c1_s, c1_r, z1_s, z1_r, sd_s, sd_r, o_s, o_r, c2_s, c2_r,
):
    n = lax.axis_index("nodes")
    c = lax.axis_index("classes")
    SL = N * CAP
    HR = RT // 2

    def znode(k):
        return lax.rem(n + k, N)

    def zfrom(k):
        return lax.rem(n - k + N, N)

    def cnode(k):
        return lax.rem(c + k, C)

    def cfrom(k):
        return lax.rem(c - k + C, C)

    xpeer = lax.rem(c + 2, C)
    kpeer = c + 1 - 2 * lax.rem(c, 2)
    xkpeer = lax.rem(kpeer + 2, C)
    order = [2, 1, 3]
    waiting = [1, 3, 2]
    PIECE = CAP // PIECES

    def remote(src, dst, s, r, **to):
        return pltpu.make_async_remote_copy(
            src_ref=src, dst_ref=dst, send_sem=s, recv_sem=r, device_id=to, device_id_type=MESH
        )

    barrier = pltpu.get_barrier_semaphore()
    for k in range(1, N):
        pl.semaphore_signal(barrier, inc=1, device_id={"nodes": znode(k)}, device_id_type=MESH)
    for k in range(1, C):
        pl.semaphore_signal(barrier, inc=1, device_id={"classes": cnode(k)}, device_id_type=MESH)

    load_scores = pltpu.make_async_copy(scores_in, scores, scores_sem)
    load_scores.start()
    own_tiles = pltpu.make_async_copy(tiles, all_tiles.at[n], local_sem)
    own_tiles.start()
    load_prior = pltpu.make_async_copy(prior_in, prior, prior_sem)
    load_prior.start()

    lane = lax.broadcasted_iota(I32, (8, 128), 1)
    line = jnp.zeros((8, 128), I32)
    for d in range(N):
        for s in range(CAP):
            line = jnp.where(lane == d * CAP + s, col_tile[0, d, s], line)
            line = jnp.where(lane == SL + d * CAP + s, row_tile[d, 0, s], line)
        line = jnp.where(lane == 2 * SL + d, counts[d], line)
    info[0:8] = line
    info[8:16] = seeds_in[...]
    rx_info[n] = info[...]

    first_end, last_end = n == 0, n == N - 1
    near = [
        jnp.where(first_end, 3, 1),
        jnp.where(jnp.logical_or(first_end, last_end), 2, 3),
        jnp.where(first_end, 1, jnp.where(last_end, 3, 2)),
    ]
    pieces = [(h, k) for h in range(PIECES) for k in near[:2]]
    pieces += [(h, near[2]) for h in range(PIECES)]

    def piece(p, q, h):
        return all_tiles.at[p, q, pl.ds(h * PIECE, PIECE)]

    def tile_up(h):
        i = h * N + 1
        return remote(
            tiles.at[c, pl.ds(h * PIECE, PIECE)], piece(n, c, h), tz_s.at[i], tz_r.at[i], nodes=up
        )

    def tile_down(h):
        i = h * N + 3
        return remote(
            tiles.at[c, pl.ds(h * PIECE, PIECE)], piece(n, c, h), tz_s.at[i], tz_r.at[i], nodes=down
        )

    up, down = lax.rem(n + 1, N), lax.rem(n + N - 1, N)

    def onward(h, k):
        p = zfrom(k)
        rising = p < n
        here = piece(p, c, h)
        to = jnp.where(rising, up, down)
        there = h * N + lax.rem(to - p + N, N)
        going = jnp.where(rising, n < N - 1, n > 0)
        return going, remote(here, here, tf_s.at[h * N + k], tz_r.at[there], nodes=to)

    def tile_x(h, k):
        i = h * N + k
        here = piece(zfrom(k), c, h)
        return remote(here, here, tx_s.at[i], tx_r.at[i], classes=xpeer)

    def tile_c(h, k):
        i = h * N + k
        here = piece(zfrom(k), c, h)
        return remote(here, here, tc_s.at[i], tc_r.at[i], classes=kpeer)

    def tile_d(h, k):
        i = h * N + k
        here = piece(zfrom(k), xpeer, h)
        return remote(here, here, td_s.at[i], td_r.at[i], classes=kpeer)

    pl.semaphore_wait(barrier, N - 1 + C - 1)
    infos = [remote(info, rx_info.at[n], info_s.at[k], info_r.at[k], nodes=znode(k)) for k in order]
    for copy in infos:
        copy.start()
    for h in range(PIECES):
        pl.when(n < N - 1)(lambda h=h: tile_up(h).start())
        pl.when(n > 0)(lambda h=h: tile_down(h).start())

    load_scores.wait()
    scs = []
    for k in order:
        d = znode(k)

        def code_scores(b, carry):
            rows = pl.ds(pl.multiple_of(d * RT, RT), RT)
            cols = pl.ds(pl.multiple_of(b * 128, 128), 128)
            words[d, b] = pack(encode_scores(scores[rows, cols]))
            return carry

        lax.fori_loop(0, NB, code_scores, 0)
        scs.append(remote(words.at[d], rx_words.at[n], sc_s.at[k], sc_r.at[k], nodes=d))
        scs[-1].start()

    own_rows = pl.ds(pl.multiple_of(n * RT, RT), RT)
    for b in range(NB):
        x = scores[own_rows, b * 128:(b + 1) * 128]
        field[n * NB + b] = x
        low[n * NB + b] = x.astype(jnp.bfloat16)

    def code_prior(d, carry):
        rows = pl.ds(pl.multiple_of(d * RT, RT), RT)
        for b in range(NB):
            pwords[d, b] = pack(
                (prior[rows, b * 128:(b + 1) * 128] * 32767.5 + 0.5).astype(I32)
            )
        return carry

    load_prior.wait()
    lax.fori_loop(0, N, code_prior, 0)
    rx_pwords[n] = pwords[n]

    txs, tcs, tds = [], [], []

    def relay_x(h, k):
        i = h * N + k
        here = piece(zfrom(k), xpeer, h)
        remote(here, here, tx_s.at[i], tx_r.at[i], classes=xpeer).wait_recv()
        tds.append(tile_d(h, k))
        tds[-1].start()

    for i, (h, k) in enumerate(pieces):
        j = h * N + k
        here = piece(zfrom(k), c, h)
        remote(here, here, tz_s.at[j], tz_r.at[j], nodes=zfrom(k)).wait_recv()
        going, copy = onward(h, k)
        pl.when(going)(copy.start)
        txs.append(tile_x(h, k))
        txs[-1].start()
        tcs.append(tile_c(h, k))
        tcs[-1].start()
        if i >= LAG:
            relay_x(*pieces[i - LAG])
    prs = [
        remote(pwords.at[znode(k)], rx_pwords.at[n], pr_s.at[k], pr_r.at[k], nodes=znode(k))
        for k in order
    ]
    for copy in prs:
        copy.start()
    for h, k in pieces[-LAG:]:
        relay_x(h, k)
    for k in order:
        remote(info, rx_info.at[zfrom(k)], info_s.at[k], info_r.at[k], nodes=zfrom(k)).wait_recv()
    to_sm = pltpu.make_async_copy(rx_info.at[:, 0:8], sm, sm_sem)
    to_sm.start()
    for k in waiting:
        p = zfrom(k)
        remote(words.at[p], rx_words.at[p], sc_s.at[k], sc_r.at[k], nodes=p).wait_recv()

        def take_scores(b, carry):
            x = decode_scores(unpack(rx_words[p, b]))
            field[p * NB + b] = x
            low[p * NB + b] = x.astype(jnp.bfloat16)
            return carry

        lax.fori_loop(0, NB, take_scores, 0)
    to_sm.wait()
    own_tiles.wait()

    def cast(p, d):
        for s in range(CAP):
            col = sm[p, 0, d * CAP + s]
            block = jnp.dot(low[p * NB + col], all_tiles[p, d, s], preferred_element_type=F32)
            votes[d * SL + p * CAP + s] = block.astype(jnp.bfloat16).astype(F32)

    def cast_from(p):
        lax.fori_loop(0, N, lambda d, carry: (cast(p, d), carry)[1], 0)

    def cast_votes(d):
        lax.fori_loop(0, N, lambda p, carry: (cast(p, d), carry)[1], 0)

    def tally(d, b):
        acc = field[d * NB + b]
        for i in range(SL):
            p, s = i // CAP, i % CAP
            row = sm[d, 0, SL + i]
            hit = jnp.logical_and(row == b, s < sm[d, 0, 2 * SL + p])
            acc = acc + jnp.where(hit, 1.0, 0.0).astype(F32) * votes[d * SL + i]
        return acc

    cast_from(n)
    for k in near:
        for h in range(PIECES):
            i = h * N + k
            here = piece(zfrom(k), kpeer, h)
            remote(here, here, tc_s.at[i], tc_r.at[i], classes=kpeer).wait_recv()
            here = piece(zfrom(k), xkpeer, h)
            remote(here, here, td_s.at[i], td_r.at[i], classes=kpeer).wait_recv()
        cast_from(zfrom(k))

    def first(d, carry):
        def one(b, carry):
            acc = tally(d, b)
            field[d * NB + b] = acc
            sums[d, pl.ds(b, 1)] = jnp.sum(acc, axis=0, keepdims=True)
            return carry

        lax.fori_loop(0, NB, one, 0)
        return carry

    lax.fori_loop(0, N, first, 0)

    rx_sums[c] = sums[...]
    c1s = [remote(sums, rx_sums.at[c], c1_s.at[k], c1_r.at[k], classes=cnode(k)) for k in range(1, C)]
    for copy in c1s:
        copy.start()
    for k in range(1, C):
        p = cfrom(k)
        remote(sums, rx_sums.at[p], c1_s.at[k], c1_r.at[k], classes=p).wait_recv()
    whole = rx_sums[0]
    for k in range(1, C):
        whole = whole + rx_sums[k]
    csums[...] = whole
    rx_csums[n] = whole
    z1s = [remote(csums, rx_csums.at[n], z1_s.at[k], z1_r.at[k], nodes=znode(k)) for k in order]
    for copy in z1s:
        copy.start()
    for k in waiting:
        p = zfrom(k)
        remote(csums, rx_csums.at[p], z1_s.at[k], z1_r.at[k], nodes=p).wait_recv()
    whole = rx_csums[0]
    for k in range(1, N):
        whole = whole + rx_csums[k]
    total[...] = 1024.0 / whole

    def spread(p):
        def one(b, carry):
            seeded = 0.5 * rx_info[p, pl.ds(8 + b, 1)].astype(F32)
            normed = field[p * NB + b] * total[p, pl.ds(b, 1)]
            seeds = unpack(rx_pwords[p, b]).astype(F32) * (1.0 / 32767.5)
            x = normed + seeded * (seeds - normed)
            field[p * NB + b] = x
            low[p * NB + b] = x.astype(jnp.bfloat16)
            return carry

        lax.fori_loop(0, NB, one, 0)

    spread(n)
    for k in waiting:
        p = zfrom(k)
        remote(pwords.at[p], rx_pwords.at[p], pr_s.at[k], pr_r.at[k], nodes=p).wait_recv()
        spread(p)

    sds, outs = [], []
    for k in order:
        d = znode(k)
        cast_votes(d)

        def one(b, carry):
            acc = tally(d, b)
            side[d, pl.ds(b, 1)] = jnp.sum(acc, axis=0, keepdims=True)
            peak = jnp.maximum(jnp.max(acc, axis=0, keepdims=True), 1e-30)
            side[d, pl.ds(8 + b, 1)] = peak * (1.0 / 65535.0)
            owords[d, b] = pack((acc * (65535.0 / peak) + 0.5).astype(I32))
            return carry

        lax.fori_loop(0, NB, one, 0)
        sds.append(remote(side.at[d], rx_side.at[n], sd_s.at[k], sd_r.at[k], nodes=d))
        outs.append(remote(owords.at[d], rx_owords.at[n], o_s.at[k], o_r.at[k], nodes=d))
        sds[-1].start()
        outs[-1].start()
    cast_votes(n)

    def own(b, carry):
        acc = tally(n, b)
        mine[b] = acc
        rx_side[n, pl.ds(b, 1)] = jnp.sum(acc, axis=0, keepdims=True)
        return carry

    lax.fori_loop(0, NB, own, 0)

    for k in waiting:
        p = zfrom(k)
        remote(side.at[p], rx_side.at[p], sd_s.at[k], sd_r.at[k], nodes=p).wait_recv()
    whole = rx_side[0, 0:8]
    for p in range(1, N):
        whole = whole + rx_side[p, 0:8]
    osum[...] = whole
    rx_osum[c] = whole
    c2s = [remote(osum, rx_osum.at[c], c2_s.at[k], c2_r.at[k], classes=cnode(k)) for k in range(1, C)]
    for copy in c2s:
        copy.start()
    for k in range(1, C):
        p = cfrom(k)
        remote(osum, rx_osum.at[p], c2_s.at[k], c2_r.at[k], classes=p).wait_recv()
    whole = rx_osum[0]
    for k in range(1, C):
        whole = whole + rx_osum[k]
    total[n] = 1024.0 / whole

    def finish(p, b, tallied):
        seeded = 0.5 * info[8 + b:9 + b].astype(F32)
        rows = pl.ds(pl.multiple_of(p * RT, RT), RT)
        normed = tallied * total[n, b:b + 1]
        out[rows, b * 128:(b + 1) * 128] = normed + seeded * (
            prior[rows, b * 128:(b + 1) * 128] - normed
        )

    for b in range(NB):
        finish(n, b, mine[b])
    for k in waiting:
        p = zfrom(k)
        remote(owords.at[p], rx_owords.at[p], o_s.at[k], o_r.at[k], nodes=p).wait_recv()
        for b in range(NB):
            codes = unpack(rx_owords[p, b]).astype(F32)
            finish(p, b, codes * rx_side[p, 8 + b:9 + b])

    for h in range(PIECES):
        pl.when(n < N - 1)(lambda h=h: tile_up(h).wait_send())
        pl.when(n > 0)(lambda h=h: tile_down(h).wait_send())
    for h, k in pieces:
        going, copy = onward(h, k)
        pl.when(going)(copy.wait_send)
    for copy in infos + scs + prs + txs + tcs + tds + c1s + z1s + sds + outs + c2s:
        copy.wait_send()


def fits(mesh, scores, tiles):
    return (
        mesh.shape["nodes"] == 4
        and mesh.shape["classes"] == 4
        and scores.shape[1] // tiles.shape[-1] == 8
        and tiles.shape[-1] == 128
        and (scores.shape[0] // 4) % 16 == 0
        and tiles.shape[2] % PIECES == 0
        and 2 * tiles.shape[1] * tiles.shape[2] + tiles.shape[1] <= 128
    )


def transposed(N, C, scores, prior, tiles, col_tile, row_tile, counts, seed_mask):
    R = scores.shape[0]
    CAP = tiles.shape[2]
    TW = tiles.shape[-1]
    NB = scores.shape[1] // TW
    RT = R // N
    SL = N * CAP
    V = pltpu.VMEM
    words = V((N, NB, RT // 2, TW), I32)
    dma = pltpu.SemaphoreType.DMA
    sems = [4] * 2 + [4 * PIECES] * 9 + [4] * 14
    pairs = [dma((size,)) for size in sems]
    smem = pl.BlockSpec(memory_space=pltpu.SMEM)
    anywhere = pl.BlockSpec(memory_space=pl.ANY)
    vm = pl.BlockSpec(memory_space=pltpu.VMEM)
    return pl.pallas_call(
        functools.partial(kernel, N, C, NB, CAP, RT),
        out_shape=jax.ShapeDtypeStruct(scores.shape, F32),
        in_specs=[anywhere] * 3 + [smem] * 3 + [vm],
        out_specs=vm,
        scratch_shapes=[
            V(scores.shape, F32), V(scores.shape, F32), V((16, TW), I32),
            words, words, words, words, words, words,
            V((N, N, CAP, TW, TW), jnp.bfloat16),
            V((N * NB, RT, TW), F32),
            V((N * NB, RT, TW), jnp.bfloat16),
            V((N * SL, RT, TW), F32),
            V((N, 16, TW), I32),
            pltpu.SMEM((N, 8, TW), I32),
            V((N, NB, TW), F32),
            V((C, N, NB, TW), F32),
            V((N, NB, TW), F32),
            V((N, N, NB, TW), F32),
            V((N, NB, TW), F32),
            V((N, 16, TW), F32),
            V((N, 16, TW), F32),
            V((NB, TW), F32),
            V((C, NB, TW), F32),
            V((NB, RT, TW), F32),
            dma, dma, dma, dma,
            *pairs,
        ],
        compiler_params=pltpu.CompilerParams(
            collective_id=0, has_side_effects=True, vmem_limit_bytes=60 * 1024 * 1024
        ),
    )(scores, prior, tiles[0], col_tile, row_tile, counts[:, 0], seed_mask.reshape(NB, TW))


def solution(mesh):
    placed = (
        P("classes", ("groups", "nodes")),
        P("classes", ("groups", "nodes")),
        P(("groups", "nodes"), None, None, None, None),
        P(("groups", "nodes"), None, None),
        P("groups", "nodes", None),
        P("groups", "nodes"),
        P(("groups", "nodes")),
    )

    def one_device(scores, prior, tiles, *rest):
        if fits(mesh, scores, tiles):
            return transposed(
                mesh.shape["nodes"], mesh.shape["classes"], scores, prior, tiles, *rest
            )
        return body(scores, prior, tiles, *rest)

    return jax.shard_map(
        one_device,
        mesh=mesh,
        in_specs=placed,
        out_specs=P("classes", ("groups", "nodes")),
        check_vma=False,
    )
```

```python
import functools

import jax
import jax.numpy as jnp
from jax import lax
from jax.experimental import pallas as pl
from jax.experimental.pallas import tpu as pltpu
from jax.sharding import PartitionSpec as P

CLASSES = 1024
ITERS = 2
MESH = pl.DeviceIdType.MESH
PIECES = 3
LAG = 3
F32 = jnp.float32
I32 = jnp.int32


def body(scores, prior, tiles, col_tile, row_tile, counts, seed_mask):
    tiles = tiles[0]
    col_tile = col_tile[0]
    incoming_rows = row_tile[:, 0]
    incoming_counts = counts[:, 0]
    tile_width = tiles.shape[-1]
    class_rows = scores.shape[0]
    block_count = scores.shape[1] // tile_width
    usable = lax.broadcasted_iota(jnp.int32, incoming_rows.shape, 1) < incoming_counts[:, None]
    target_pick = jax.nn.one_hot(incoming_rows, block_count, dtype=jnp.bfloat16) * usable[
        ..., None
    ].astype(jnp.bfloat16)
    source_pick = jax.nn.one_hot(col_tile, block_count, dtype=jnp.bfloat16)
    seeded = seed_mask.astype(jnp.float32)[None, :]
    scores_now = scores
    for sweep in range(ITERS):
        field_low = scores_now.astype(jnp.bfloat16).reshape(class_rows, block_count, tile_width)
        picked = jnp.einsum(
            "pse,cek->psck", source_pick, field_low, preferred_element_type=jnp.float32
        ).astype(jnp.bfloat16)
        products = jnp.einsum(
            "psck,pskj->pscj", picked, tiles, preferred_element_type=jnp.float32
        ).astype(jnp.bfloat16)
        arrived = lax.all_to_all(products, "nodes", split_axis=0, concat_axis=0, tiled=True)
        gathered = jnp.einsum(
            "pse,pscj->cej", target_pick, arrived, preferred_element_type=jnp.float32
        )
        tallied = scores_now + gathered.reshape(class_rows, block_count * tile_width)
        node_total = lax.psum(jnp.sum(tallied, axis=0), "classes")
        normed = CLASSES * tallied / node_total[None, :]
        scores_now = normed + 0.5 * seeded * (prior - normed)
    return scores_now


def pack(codes):
    half = codes.shape[0] // 2
    return lax.bitwise_or(codes[:half], lax.shift_left(codes[half:], jnp.int32(16)))


def unpack(words):
    low = lax.bitwise_and(words, jnp.int32(0xFFFF))
    high = lax.shift_right_logical(words, jnp.int32(16))
    return jnp.concatenate([low, high], axis=0)


def encode_scores(x):
    step = jnp.full_like(x, 65536.0)
    octave = jnp.full(x.shape, -8192, I32)
    edge, scale = 0.25, 32768.0
    for level in range(7):
        above = x >= edge
        step = jnp.where(above, scale, step)
        octave = jnp.where(above, level * 8192, octave)
        edge, scale = edge * 2.0, scale * 0.5
    return (x * step).astype(I32) + octave


def decode_scores(codes):
    octave = lax.shift_right_logical(codes, jnp.int32(13))
    mantissa = lax.bitwise_and(codes, jnp.int32(8191)).astype(F32) + 8192.5
    power = lax.shift_left(jnp.full_like(codes, 1), octave).astype(F32)
    return mantissa * (power * (1.0 / 65536.0))


def kernel(
    N, C, NB, CAP, RT,
    scores_in, prior_in, tiles, col_tile, row_tile, counts, seeds_in, out,
    scores, prior, info,
    words, rx_words, pwords, rx_pwords, owords, rx_owords,
    all_tiles, field, low, votes, rx_info, sm,
    sums, rx_sums, csums, rx_csums, total, side, rx_side, osum, rx_osum, mine,
    local_sem, scores_sem, prior_sem, sm_sem,
    info_s, info_r, tz_s, tz_r, tf_s, tx_s, tx_r, tc_s, tc_r, td_s, td_r,
    sc_s, sc_r, pr_s, pr_r, c1_s, c1_r, z1_s, z1_r, sd_s, sd_r, o_s, o_r, c2_s, c2_r,
):
    n = lax.axis_index("nodes")
    c = lax.axis_index("classes")
    SL = N * CAP
    HR = RT // 2

    def znode(k):
        return lax.rem(n + k, N)

    def zfrom(k):
        return lax.rem(n - k + N, N)

    def cnode(k):
        return lax.rem(c + k, C)

    def cfrom(k):
        return lax.rem(c - k + C, C)

    xpeer = lax.rem(c + 2, C)
    kpeer = c + 1 - 2 * lax.rem(c, 2)
    xkpeer = lax.rem(kpeer + 2, C)
    order = [2, 1, 3]
    waiting = [1, 3, 2]
    PIECE = CAP // PIECES

    def remote(src, dst, s, r, **to):
        return pltpu.make_async_remote_copy(
            src_ref=src, dst_ref=dst, send_sem=s, recv_sem=r, device_id=to, device_id_type=MESH
        )

    barrier = pltpu.get_barrier_semaphore()
    for k in range(1, N):
        pl.semaphore_signal(barrier, inc=1, device_id={"nodes": znode(k)}, device_id_type=MESH)
    for k in range(1, C):
        pl.semaphore_signal(barrier, inc=1, device_id={"classes": cnode(k)}, device_id_type=MESH)

    load_scores = pltpu.make_async_copy(scores_in, scores, scores_sem)
    load_scores.start()
    own_tiles = pltpu.make_async_copy(tiles, all_tiles.at[n], local_sem)
    own_tiles.start()
    load_prior = pltpu.make_async_copy(prior_in, prior, prior_sem)
    load_prior.start()

    lane = lax.broadcasted_iota(I32, (8, 128), 1)
    line = jnp.zeros((8, 128), I32)
    for d in range(N):
        for s in range(CAP):
            line = jnp.where(lane == d * CAP + s, col_tile[0, d, s], line)
            line = jnp.where(lane == SL + d * CAP + s, row_tile[d, 0, s], line)
        line = jnp.where(lane == 2 * SL + d, counts[d], line)
    info[0:8] = line
    info[8:16] = seeds_in[...]
    rx_info[n] = info[...]

    first_end, last_end = n == 0, n == N - 1
    near = [
        jnp.where(first_end, 3, 1),
        jnp.where(jnp.logical_or(first_end, last_end), 2, 3),
        jnp.where(first_end, 1, jnp.where(last_end, 3, 2)),
    ]
    pieces = [(h, k) for h in range(PIECES) for k in near[:2]]
    pieces += [(h, near[2]) for h in range(PIECES)]

    def piece(p, q, h):
        return all_tiles.at[p, q, pl.ds(h * PIECE, PIECE)]

    def tile_up(h):
        i = h * N + 1
        return remote(
            tiles.at[c, pl.ds(h * PIECE, PIECE)], piece(n, c, h), tz_s.at[i], tz_r.at[i], nodes=up
        )

    def tile_down(h):
        i = h * N + 3
        return remote(
            tiles.at[c, pl.ds(h * PIECE, PIECE)], piece(n, c, h), tz_s.at[i], tz_r.at[i], nodes=down
        )

    up, down = lax.rem(n + 1, N), lax.rem(n + N - 1, N)

    def onward(h, k):
        p = zfrom(k)
        rising = p < n
        here = piece(p, c, h)
        to = jnp.where(rising, up, down)
        there = h * N + lax.rem(to - p + N, N)
        going = jnp.where(rising, n < N - 1, n > 0)
        return going, remote(here, here, tf_s.at[h * N + k], tz_r.at[there], nodes=to)

    def tile_x(h, k):
        i = h * N + k
        here = piece(zfrom(k), c, h)
        return remote(here, here, tx_s.at[i], tx_r.at[i], classes=xpeer)

    def tile_c(h, k):
        i = h * N + k
        here = piece(zfrom(k), c, h)
        return remote(here, here, tc_s.at[i], tc_r.at[i], classes=kpeer)

    def tile_d(h, k):
        i = h * N + k
        here = piece(zfrom(k), xpeer, h)
        return remote(here, here, td_s.at[i], td_r.at[i], classes=kpeer)

    pl.semaphore_wait(barrier, N - 1 + C - 1)
    infos = [remote(info, rx_info.at[n], info_s.at[k], info_r.at[k], nodes=znode(k)) for k in order]
    for copy in infos:
        copy.start()
    for h in range(PIECES):
        pl.when(n < N - 1)(lambda h=h: tile_up(h).start())
        pl.when(n > 0)(lambda h=h: tile_down(h).start())

    load_scores.wait()
    scs = []
    for k in order:
        d = znode(k)

        def code_scores(b, carry):
            rows = pl.ds(pl.multiple_of(d * RT, RT), RT)
            cols = pl.ds(pl.multiple_of(b * 128, 128), 128)
            words[d, b] = pack(encode_scores(scores[rows, cols]))
            return carry

        lax.fori_loop(0, NB, code_scores, 0)
        scs.append(remote(words.at[d], rx_words.at[n], sc_s.at[k], sc_r.at[k], nodes=d))
        scs[-1].start()

    own_rows = pl.ds(pl.multiple_of(n * RT, RT), RT)
    for b in range(NB):
        x = scores[own_rows, b * 128:(b + 1) * 128]
        field[n * NB + b] = x
        low[n * NB + b] = x.astype(jnp.bfloat16)

    def code_prior(d, carry):
        rows = pl.ds(pl.multiple_of(d * RT, RT), RT)
        for b in range(NB):
            pwords[d, b] = pack(
                (prior[rows, b * 128:(b + 1) * 128] * 32767.5 + 0.5).astype(I32)
            )
        return carry

    load_prior.wait()
    lax.fori_loop(0, N, code_prior, 0)
    rx_pwords[n] = pwords[n]

    txs, tcs, tds = [], [], []

    def relay_x(h, k):
        i = h * N + k
        here = piece(zfrom(k), xpeer, h)
        remote(here, here, tx_s.at[i], tx_r.at[i], classes=xpeer).wait_recv()
        tds.append(tile_d(h, k))
        tds[-1].start()

    for i, (h, k) in enumerate(pieces):
        j = h * N + k
        here = piece(zfrom(k), c, h)
        remote(here, here, tz_s.at[j], tz_r.at[j], nodes=zfrom(k)).wait_recv()
        going, copy = onward(h, k)
        pl.when(going)(copy.start)
        txs.append(tile_x(h, k))
        txs[-1].start()
        tcs.append(tile_c(h, k))
        tcs[-1].start()
        if i >= LAG:
            relay_x(*pieces[i - LAG])
    for h, k in pieces[-LAG:]:
        relay_x(h, k)
    for k in order:
        remote(info, rx_info.at[zfrom(k)], info_s.at[k], info_r.at[k], nodes=zfrom(k)).wait_recv()
    to_sm = pltpu.make_async_copy(rx_info.at[:, 0:8], sm, sm_sem)
    to_sm.start()
    for k in waiting:
        p = zfrom(k)
        remote(words.at[p], rx_words.at[p], sc_s.at[k], sc_r.at[k], nodes=p).wait_recv()

        def take_scores(b, carry):
            x = decode_scores(unpack(rx_words[p, b]))
            field[p * NB + b] = x
            low[p * NB + b] = x.astype(jnp.bfloat16)
            return carry

        lax.fori_loop(0, NB, take_scores, 0)
    prs = [
        remote(pwords.at[znode(k)], rx_pwords.at[n], pr_s.at[k], pr_r.at[k], nodes=znode(k))
        for k in order
    ]
    for copy in prs:
        copy.start()
    to_sm.wait()
    own_tiles.wait()

    def cast(p, d):
        for s in range(CAP):
            col = sm[p, 0, d * CAP + s]
            block = jnp.dot(low[p * NB + col], all_tiles[p, d, s], preferred_element_type=F32)
            votes[d * SL + p * CAP + s] = block.astype(jnp.bfloat16).astype(F32)

    def cast_from(p):
        lax.fori_loop(0, N, lambda d, carry: (cast(p, d), carry)[1], 0, unroll=True)

    def cast_votes(d):
        lax.fori_loop(0, N, lambda p, carry: (cast(p, d), carry)[1], 0, unroll=True)

    def tally(d, b):
        acc = field[d * NB + b]
        for i in range(SL):
            p, s = i // CAP, i % CAP
            row = sm[d, 0, SL + i]
            hit = jnp.logical_and(row == b, s < sm[d, 0, 2 * SL + p])
            acc = acc + jnp.where(hit, 1.0, 0.0).astype(F32) * votes[d * SL + i]
        return acc

    cast_from(n)
    for k in near:
        for h in range(PIECES):
            i = h * N + k
            here = piece(zfrom(k), kpeer, h)
            remote(here, here, tc_s.at[i], tc_r.at[i], classes=kpeer).wait_recv()
            here = piece(zfrom(k), xkpeer, h)
            remote(here, here, td_s.at[i], td_r.at[i], classes=kpeer).wait_recv()
        cast_from(zfrom(k))

    def first(d, carry):
        def one(b, carry):
            acc = tally(d, b)
            field[d * NB + b] = acc
            sums[d, pl.ds(b, 1)] = jnp.sum(acc, axis=0, keepdims=True)
            return carry

        lax.fori_loop(0, NB, one, 0)
        return carry

    lax.fori_loop(0, N, first, 0)

    rx_sums[c] = sums[...]
    c1s = [remote(sums, rx_sums.at[c], c1_s.at[k], c1_r.at[k], classes=cnode(k)) for k in range(1, C)]
    for copy in c1s:
        copy.start()
    for k in range(1, C):
        p = cfrom(k)
        remote(sums, rx_sums.at[p], c1_s.at[k], c1_r.at[k], classes=p).wait_recv()
    whole = rx_sums[0]
    for k in range(1, C):
        whole = whole + rx_sums[k]
    csums[...] = whole
    rx_csums[n] = whole
    z1s = [remote(csums, rx_csums.at[n], z1_s.at[k], z1_r.at[k], nodes=znode(k)) for k in order]
    for copy in z1s:
        copy.start()
    for k in waiting:
        p = zfrom(k)
        remote(csums, rx_csums.at[p], z1_s.at[k], z1_r.at[k], nodes=p).wait_recv()
    whole = rx_csums[0]
    for k in range(1, N):
        whole = whole + rx_csums[k]
    total[...] = 1024.0 / whole

    def spread(p):
        def one(b, carry):
            seeded = 0.5 * rx_info[p, pl.ds(8 + b, 1)].astype(F32)
            normed = field[p * NB + b] * total[p, pl.ds(b, 1)]
            seeds = unpack(rx_pwords[p, b]).astype(F32) * (1.0 / 32767.5)
            x = normed + seeded * (seeds - normed)
            field[p * NB + b] = x
            low[p * NB + b] = x.astype(jnp.bfloat16)
            return carry

        lax.fori_loop(0, NB, one, 0)

    spread(n)
    for k in waiting:
        p = zfrom(k)
        remote(pwords.at[p], rx_pwords.at[p], pr_s.at[k], pr_r.at[k], nodes=p).wait_recv()
        spread(p)

    sds, outs = [], []
    for k in order:
        d = znode(k)
        cast_votes(d)

        def one(b, carry):
            acc = tally(d, b)
            side[d, pl.ds(b, 1)] = jnp.sum(acc, axis=0, keepdims=True)
            peak = jnp.maximum(jnp.max(acc, axis=0, keepdims=True), 1e-30)
            side[d, pl.ds(8 + b, 1)] = peak * (1.0 / 65535.0)
            owords[d, b] = pack((acc * (65535.0 / peak) + 0.5).astype(I32))
            return carry

        lax.fori_loop(0, NB, one, 0)
        sds.append(remote(side.at[d], rx_side.at[n], sd_s.at[k], sd_r.at[k], nodes=d))
        outs.append(remote(owords.at[d], rx_owords.at[n], o_s.at[k], o_r.at[k], nodes=d))
        sds[-1].start()
        outs[-1].start()
    cast_votes(n)

    def own(b, carry):
        acc = tally(n, b)
        mine[b] = acc
        rx_side[n, pl.ds(b, 1)] = jnp.sum(acc, axis=0, keepdims=True)
        return carry

    lax.fori_loop(0, NB, own, 0)

    for k in waiting:
        p = zfrom(k)
        remote(side.at[p], rx_side.at[p], sd_s.at[k], sd_r.at[k], nodes=p).wait_recv()
    whole = rx_side[0, 0:8]
    for p in range(1, N):
        whole = whole + rx_side[p, 0:8]
    osum[...] = whole
    rx_osum[c] = whole
    c2s = [remote(osum, rx_osum.at[c], c2_s.at[k], c2_r.at[k], classes=cnode(k)) for k in range(1, C)]
    for copy in c2s:
        copy.start()
    for k in range(1, C):
        p = cfrom(k)
        remote(osum, rx_osum.at[p], c2_s.at[k], c2_r.at[k], classes=p).wait_recv()
    whole = rx_osum[0]
    for k in range(1, C):
        whole = whole + rx_osum[k]
    total[n] = 1024.0 / whole

    def finish(p, b, tallied):
        seeded = 0.5 * info[8 + b:9 + b].astype(F32)
        rows = pl.ds(pl.multiple_of(p * RT, RT), RT)
        normed = tallied * total[n, b:b + 1]
        out[rows, b * 128:(b + 1) * 128] = normed + seeded * (
            prior[rows, b * 128:(b + 1) * 128] - normed
        )

    for b in range(NB):
        finish(n, b, mine[b])
    for k in waiting:
        p = zfrom(k)
        remote(owords.at[p], rx_owords.at[p], o_s.at[k], o_r.at[k], nodes=p).wait_recv()
        for b in range(NB):
            codes = unpack(rx_owords[p, b]).astype(F32)
            finish(p, b, codes * rx_side[p, 8 + b:9 + b])

    for h in range(PIECES):
        pl.when(n < N - 1)(lambda h=h: tile_up(h).wait_send())
        pl.when(n > 0)(lambda h=h: tile_down(h).wait_send())
    for h, k in pieces:
        going, copy = onward(h, k)
        pl.when(going)(copy.wait_send)
    for copy in infos + scs + prs + txs + tcs + tds + c1s + z1s + sds + outs + c2s:
        copy.wait_send()


def fits(mesh, scores, tiles):
    return (
        mesh.shape["nodes"] == 4
        and mesh.shape["classes"] == 4
        and scores.shape[1] // tiles.shape[-1] == 8
        and tiles.shape[-1] == 128
        and (scores.shape[0] // 4) % 16 == 0
        and tiles.shape[2] % PIECES == 0
        and 2 * tiles.shape[1] * tiles.shape[2] + tiles.shape[1] <= 128
    )


def transposed(N, C, scores, prior, tiles, col_tile, row_tile, counts, seed_mask):
    R = scores.shape[0]
    CAP = tiles.shape[2]
    TW = tiles.shape[-1]
    NB = scores.shape[1] // TW
    RT = R // N
    SL = N * CAP
    V = pltpu.VMEM
    words = V((N, NB, RT // 2, TW), I32)
    dma = pltpu.SemaphoreType.DMA
    sems = [4] * 2 + [4 * PIECES] * 9 + [4] * 14
    pairs = [dma((size,)) for size in sems]
    smem = pl.BlockSpec(memory_space=pltpu.SMEM)
    anywhere = pl.BlockSpec(memory_space=pl.ANY)
    vm = pl.BlockSpec(memory_space=pltpu.VMEM)
    return pl.pallas_call(
        functools.partial(kernel, N, C, NB, CAP, RT),
        out_shape=jax.ShapeDtypeStruct(scores.shape, F32),
        in_specs=[anywhere] * 3 + [smem] * 3 + [vm],
        out_specs=vm,
        scratch_shapes=[
            V(scores.shape, F32), V(scores.shape, F32), V((16, TW), I32),
            words, words, words, words, words, words,
            V((N, N, CAP, TW, TW), jnp.bfloat16),
            V((N * NB, RT, TW), F32),
            V((N * NB, RT, TW), jnp.bfloat16),
            V((N * SL, RT, TW), F32),
            V((N, 16, TW), I32),
            pltpu.SMEM((N, 8, TW), I32),
            V((N, NB, TW), F32),
            V((C, N, NB, TW), F32),
            V((N, NB, TW), F32),
            V((N, N, NB, TW), F32),
            V((N, NB, TW), F32),
            V((N, 16, TW), F32),
            V((N, 16, TW), F32),
            V((NB, TW), F32),
            V((C, NB, TW), F32),
            V((NB, RT, TW), F32),
            dma, dma, dma, dma,
            *pairs,
        ],
        compiler_params=pltpu.CompilerParams(
            collective_id=0, has_side_effects=True, vmem_limit_bytes=60 * 1024 * 1024
        ),
    )(scores, prior, tiles[0], col_tile, row_tile, counts[:, 0], seed_mask.reshape(NB, TW))


def solution(mesh):
    placed = (
        P("classes", ("groups", "nodes")),
        P("classes", ("groups", "nodes")),
        P(("groups", "nodes"), None, None, None, None),
        P(("groups", "nodes"), None, None),
        P("groups", "nodes", None),
        P("groups", "nodes"),
        P(("groups", "nodes")),
    )

    def one_device(scores, prior, tiles, *rest):
        if fits(mesh, scores, tiles):
            return transposed(
                mesh.shape["nodes"], mesh.shape["classes"], scores, prior, tiles, *rest
            )
        return body(scores, prior, tiles, *rest)

    return jax.shard_map(
        one_device,
        mesh=mesh,
        in_specs=placed,
        out_specs=P("classes", ("groups", "nodes")),
        check_vma=False,
    )
```
